32 devices in a mesh: row: 16 (over z, x, core), col: 2 (over y).
Axes of the slice: x: 2, y: 2, z: 4, core: 2. Of those that a mesh axis runs over, the one named last changes fastest.
Arguments:
- tensor: bfloat16 [1024, 512, 256], P('row', 'col'), may hold values from -8.808155 to 8.808155
- factor_a: float32 [1024, 256], P(('row', 'col')), may hold values from -0.59375 to 0.59375
- factor_b: float32 [512, 256], P(('col', 'row')), may hold values from -0.8396893 to 0.8396893
- factor_c: float32 [256, 256], replicated, may hold values from -1.1875 to 1.1875
Outputs:
- grad_a: float32 [1024, 256], P(('row', 'col'))
- grad_b: float32 [512, 256], P(('col', 'row'))
- grad_c: float32 [256, 256], replicated
The draws below stay inside these ranges and needn't reach their ends.
All inputs are finite; a program needn't handle non-finite values.
Results may differ from the reference program's by a relative error of at most 0.0018.
Values sent between devices are 32-bit elements; how exact they have to be, the bound alone decides.
A program may use at most 128 MiB of HBM per device.

```python
import jax
import jax.numpy as jnp
from jax import lax

R = 256
K = 256
IB = 64
I = 1024
J = 512
N_ROW = 16


def row_rise(count):
    place = jnp.arange(count, dtype=jnp.float32) / count - 0.5
    return jnp.exp(jnp.log(3.0) * place) * (2.0 / count ** 0.5)


def mixed_values(key, shape, normal_weight, normal_clip):
    first = jax.random.fold_in(key, 0)
    normal_part = jnp.clip(jax.random.normal(first, shape, jnp.float32), -normal_clip, normal_clip)
    return normal_weight * normal_part


def shared_part(key, salt, count, level_mix):
    key = jax.random.fold_in(key, salt)
    level = mixed_values(key, (count,), level_mix[0], 2.5)
    return level * row_rise(count)


def factor_rows(key, count, base_mix, common):
    base = mixed_values(key, (count, R), base_mix[0], 4.0)
    return base * row_rise(count)[:, None] + common[:, None]


def draw_factor_a(key, part):
    level_mix = (0.5, 0.0, 0.0)
    base_mix = (1.0, 0.0, 0.0)
    common = shared_part(key, 31, I, level_mix)
    key = jax.random.fold_in(key, 11)
    return factor_rows(key, I, base_mix, common)


def draw_factor_b(key, part):
    level_mix = (0.5, 0.0, 0.0)
    base_mix = (1.0, 0.0, 0.0)
    common = shared_part(key, 37, J, level_mix)
    key = jax.random.fold_in(key, 23)
    return factor_rows(key, J, base_mix, common)


def draw_factor_c(key, part):
    level_mix = (0.5, 0.0, 0.0)
    base_mix = (1.0, 0.0, 0.0)
    common = shared_part(key, 41, K, level_mix)
    key = jax.random.fold_in(key, 29)
    return factor_rows(key, K, base_mix, common)


def draw_tensor(key, part):
    level_mix = (0.5, 0.0, 0.0)
    first = shared_part(key, 31, I, level_mix)
    second = shared_part(key, 37, J, level_mix)
    third = shared_part(key, 41, K, level_mix)
    key = jax.random.fold_in(key, 5)
    noise = jnp.clip(0.3 * jax.random.normal(key, (I, J, K), jnp.float32), -2.4, 2.4)
    model = 0.85 * R * first[:, None, None] * second[None, :, None] * third[None, None, :]
    return (model + noise).astype(jnp.bfloat16)


def setup_inputs(seed: int = 0) -> dict:
    streams_of = jax.random.split(jax.random.key(seed), 5)
    return {
        "tensor": draw_tensor(jax.random.fold_in(streams_of[4], 71), 0),
        "factor_a": draw_factor_a(jax.random.fold_in(streams_of[4], 71), 0),
        "factor_b": draw_factor_b(jax.random.fold_in(streams_of[4], 71), 0),
        "factor_c": draw_factor_c(jax.random.fold_in(streams_of[4], 71), 0),
    }


def reference(tensor, factor_a, factor_b, factor_c):
    highest = lax.Precision.HIGHEST
    gram_a = jnp.dot(factor_a.T, factor_a, precision=highest)
    gram_b = jnp.dot(factor_b.T, factor_b, precision=highest)
    gram_c = jnp.dot(factor_c.T, factor_c, precision=highest)
    c_low = lax.optimization_barrier(factor_c.astype(jnp.bfloat16)).astype(jnp.float32)
    blocks = tensor.reshape(N_ROW, IB, J, K)
    a_blocks = factor_a.reshape(N_ROW, IB, R)

    def one_block(inputs):
        block, a_part = inputs
        block_f = block.astype(jnp.float32)
        contracted = jnp.einsum("ijk,kr->ijr", block_f, c_low, precision=highest)
        part_a = jnp.einsum("ijr,jr->ir", contracted, factor_b, precision=highest)
        part_b = jnp.einsum("ijr,ir->jr", contracted, a_part, precision=highest)
        panel = a_part[:, None, :] * factor_b[None, :, :]
        panel = lax.optimization_barrier(panel.astype(jnp.bfloat16)).astype(jnp.float32)
        part_c = jnp.dot(block_f.reshape(IB * J, K).T, panel.reshape(IB * J, R), precision=highest)
        return part_a, part_b, part_c

    parts_a, parts_b, parts_c = lax.map(one_block, (blocks, a_blocks))
    mttkrp_a = parts_a.reshape(I, R)
    mttkrp_b = jnp.sum(parts_b, axis=0)
    mttkrp_c = jnp.sum(parts_c, axis=0)
    grad_a = jnp.dot(factor_a, gram_b * gram_c, precision=highest) - mttkrp_a
    grad_b = jnp.dot(factor_b, gram_a * gram_c, precision=highest) - mttkrp_b
    grad_c = jnp.dot(factor_c, gram_a * gram_b, precision=highest) - mttkrp_c
    return (grad_a, grad_b, grad_c)
```

```python
import functools

import jax
import jax.numpy as jnp
from jax import lax
from jax.experimental import pallas as pl
from jax.experimental.pallas import tpu as pltpu
from jax.sharding import PartitionSpec as P

MESH = pl.DeviceIdType.MESH
HIGHEST = lax.Precision.HIGHEST
GROUP = 4


def dot(left, right):
    return jnp.dot(left, right, precision=HIGHEST, preferred_element_type=jnp.float32)


def kernel(
    n_row, n_col,
    t_hbm, fa_ref, fb_ref, fc_ref,
    out_a, out_b, out_c,
    t_ref, x_ref, a_gather, b_gather, a_ref, c_low, gram_c,
    part_ga, part_mb, part_mc, mate_ga, mate_mb, mate_mc, half_ga, half_mb, half_mc,
    peer_ga, peer_mb, peer_mc, col_ma, col_gb, col_mc, part_gb, part_ma,
    grams, final_c,
    load_sem, row_send, row_recv, mate_send, mate_recv, col_send, col_recv,
):
    row, col = lax.axis_index("row"), lax.axis_index("col")
    chips = n_row // 2
    chip, core = row // 2, lax.rem(row, 2)
    mate = {"row": row + 1 - 2 * core}
    rows_i, rows_j, depth = t_ref.shape
    rank = fa_ref.shape[1]
    own_a, own_b = fa_ref.shape[0], fb_ref.shape[0]
    steps = rows_i // GROUP
    sends = []

    def at_chip(shift):
        return lax.rem(chip + shift, chips)

    def across_row(phase, source, target):
        def copies():
            for shift in range(1, chips):
                other = at_chip(shift)
                yield pltpu.make_async_remote_copy(
                    src_ref=source(other), dst_ref=target,
                    send_sem=row_send.at[phase, shift], recv_sem=row_recv.at[phase, shift],
                    device_id={"row": 2 * other + core}, device_id_type=MESH,
                )
        made = list(copies())
        for copy in made:
            copy.start()
        sends.extend(made)
        return made

    def across_mate(phase, source, target):
        copy = pltpu.make_async_remote_copy(
            src_ref=source, dst_ref=target,
            send_sem=mate_send.at[phase], recv_sem=mate_recv.at[phase],
            device_id=mate, device_id_type=MESH,
        )
        copy.start()
        sends.append(copy)
        return [copy]

    def across_col(phase, source, target):
        made = []
        for shift in range(1, n_col):
            other = lax.rem(col + shift, n_col)
            copy = pltpu.make_async_remote_copy(
                src_ref=source(other), dst_ref=target,
                send_sem=col_send.at[phase, shift], recv_sem=col_recv.at[phase, shift],
                device_id={"col": other}, device_id_type=MESH,
            )
            copy.start()
            made.append(copy)
        sends.extend(made)
        return made

    def arrive(made):
        for copy in made:
            copy.wait_recv()

    def load(step):
        part = pl.ds(step * GROUP, GROUP)
        return pltpu.make_async_copy(t_hbm.at[part], t_ref.at[part], load_sem.at[step])

    for step in range(steps):
        load(step).start()

    barrier = pltpu.get_barrier_semaphore()
    pl.semaphore_signal(barrier, inc=1, device_id=mate, device_id_type=MESH)
    for shift in range(1, chips):
        pl.semaphore_signal(
            barrier, inc=1, device_id={"row": 2 * at_chip(shift) + core}, device_id_type=MESH
        )
    for shift in range(1, n_col):
        pl.semaphore_signal(
            barrier, inc=1, device_id={"col": lax.rem(col + shift, n_col)}, device_id_type=MESH
        )
    a_gather[col] = fa_ref[...]
    b_gather[chip, core] = fb_ref[...]
    pl.semaphore_wait(barrier, chips + n_col - 1)

    a_moves = across_col(0, lambda other: a_gather.at[col], a_gather.at[col])
    b_moves = across_row(0, lambda other: b_gather.at[chip, core], b_gather.at[chip, core])
    factor_c = fc_ref[...]
    c_low[...] = factor_c.astype(jnp.bfloat16)
    gram_c[...] = dot(factor_c.T, factor_c)
    part_mb[...] = jnp.zeros_like(part_mb)
    part_mc[...] = jnp.zeros_like(part_mc)
    arrive(a_moves)
    a_block = a_gather[...].reshape(rows_i, rank)
    a_ref[...] = a_block
    part_ga[...] = dot(a_block.T, a_block).reshape(part_ga.shape)
    ga_mate = across_mate(0, part_ga.at[:, 1 - core], mate_ga)

    def first_pass(begin, end):
        @pl.loop(begin, end)
        def _(step):
            load(step).wait()
            base = step * GROUP
            flat = t_ref[pl.ds(base, GROUP)].reshape(GROUP * rows_j, depth)
            product = jnp.dot(flat, c_low[...], preferred_element_type=jnp.float32)
            product = product.reshape(GROUP, rows_j, rank)
            x_ref[pl.ds(base, GROUP)] = product
            total = part_mb[...].reshape(rows_j, rank)
            for i in range(GROUP):
                total += product[i] * a_ref[pl.ds(base + i, 1), :]
            part_mb[...] = total.reshape(part_mb.shape)

    def second_pass(begin, end):
        @pl.loop(begin, end)
        def _(step):
            base = step * GROUP
            b_block = b_gather[...].reshape(rows_j, rank)
            panels = []
            for i in range(GROUP):
                a_row = a_ref[pl.ds(base + i, 1), :]
                panels.append((a_row * b_block).astype(jnp.bfloat16))
                part_ma[pl.ds(base + i, 1), :] = jnp.sum(
                    x_ref[base + i] * b_block, axis=0, keepdims=True
                )
            panel = jnp.concatenate(panels, axis=0)
            flat = t_ref[pl.ds(base, GROUP)].reshape(GROUP * rows_j, depth)
            product = lax.dot_general(
                flat, panel, (((0,), (0,)), ((), ())), preferred_element_type=jnp.float32
            )
            part_mc[...] += product.reshape(part_mc.shape)

    first_pass(0, steps // 2)
    arrive(ga_mate)
    half_ga[...] = part_ga[:, core] + mate_ga[...]
    ga_moves = across_row(1, lambda other: half_ga.at[other], peer_ga.at[chip])
    peer_ga[chip] = half_ga[chip]
    arrive(b_moves)
    b_mate = across_mate(1, b_gather.at[:, core], b_gather.at[:, core])
    first_pass(steps // 2, steps)
    mb_mate = across_mate(2, part_mb.at[:, 1 - core], mate_mb)
    arrive(b_mate)
    b_block = b_gather[...].reshape(rows_j, rank)
    part_gb[...] = dot(b_block.T, b_block).reshape(part_gb.shape)
    col_gb[col] = part_gb[row]
    gb_moves = across_col(1, lambda other: part_gb.at[row], col_gb.at[col])
    second_pass(0, steps // 4)
    arrive(mb_mate)
    half_mb[...] = part_mb[:, core] + mate_mb[...]
    mb_moves = across_row(2, lambda other: half_mb.at[other], peer_mb.at[chip])
    peer_mb[chip] = half_mb[chip]
    arrive(ga_moves)
    arrive(gb_moves)
    gram_rows = [jnp.sum(peer_ga[...], axis=0), jnp.sum(col_gb[...], axis=0)]
    grams[chip, core] = jnp.stack(gram_rows)
    gram_moves = across_row(3, lambda other: grams.at[chip, core], grams.at[chip, core])
    second_pass(steps // 4, steps)

    mc_mate = across_mate(3, part_mc.at[:, 1 - core], mate_mc)
    ma_moves = across_col(
        2,
        lambda other: part_ma.at[pl.ds(pl.multiple_of(other * own_a, 8), own_a)],
        col_ma.at[col],
    )
    col_ma[col] = part_ma[pl.ds(pl.multiple_of(col * own_a, 8), own_a), :]
    arrive(gram_moves)
    gram_mate = across_mate(4, grams.at[:, core], grams.at[:, core])
    arrive(mc_mate)
    half_mc[...] = part_mc[:, core] + mate_mc[...]
    mc_moves = across_row(4, lambda other: half_mc.at[other], peer_mc.at[chip])
    peer_mc[chip] = half_mc[chip]
    arrive(gram_mate)
    gram_a = grams[:, :, 0].reshape(rank, rank)
    gram_b = grams[:, :, 1].reshape(rank, rank)
    slice_c = depth // n_row
    rows_c = fc_ref[pl.ds(pl.multiple_of(row * slice_c, 8), slice_c), :]
    model_c = dot(rows_c, gram_a * gram_b)
    arrive(mc_moves)
    total_c = jnp.sum(peer_mc[...], axis=0)
    col_mc[col] = total_c
    c_moves = across_col(3, lambda other: col_mc.at[col], col_mc.at[col])
    model_a = dot(fa_ref[...], gram_b * gram_c[...])
    model_b = dot(fb_ref[...], gram_a * gram_c[...])
    arrive(c_moves)
    final_c[chip, core] = model_c - jnp.sum(col_mc[...], axis=0)
    final_moves = across_row(5, lambda other: final_c.at[chip, core], final_c.at[chip, core])
    arrive(ma_moves)
    out_a[...] = model_a - jnp.sum(col_ma[...], axis=0)
    arrive(mb_moves)
    out_b[...] = model_b - jnp.sum(peer_mb[...], axis=0)
    arrive(final_moves)
    final_mate = across_mate(5, final_c.at[:, core], final_c.at[:, core])
    arrive(final_mate)
    out_c[...] = final_c[...]
    for copy in sends:
        copy.wait_send()


def shards(n_row, n_col, tensor, factor_a, factor_b, factor_c):
    rows_i, rows_j, depth = tensor.shape
    own_a, rank = factor_a.shape
    own_b = factor_b.shape[0]
    chips = n_row // 2
    part_r, part_k = rank // n_row, depth // n_row
    f32 = jnp.float32

    def buffer(*shape):
        return pltpu.VMEM(shape + (rank,), f32)

    vmem = pl.BlockSpec(memory_space=pltpu.VMEM)
    grad_a, grad_b, grad_c = pl.pallas_call(
        functools.partial(kernel, n_row, n_col),
        out_shape=(
            jax.ShapeDtypeStruct((own_a, rank), f32),
            jax.ShapeDtypeStruct((own_b, rank), f32),
            jax.ShapeDtypeStruct((chips, 2, part_k, rank), f32),
        ),
        in_specs=[pl.BlockSpec(memory_space=pl.ANY), vmem, vmem, vmem],
        out_specs=(vmem, vmem, vmem),
        scratch_shapes=[
            pltpu.VMEM(tensor.shape, tensor.dtype),
            buffer(rows_i, rows_j),
            buffer(n_col, own_a),
            buffer(chips, 2, own_b),
            buffer(rows_i),
            pltpu.VMEM((depth, rank), jnp.bfloat16),
            buffer(rank),
            buffer(chips, 2, part_r), buffer(chips, 2, own_b), buffer(chips, 2, part_k),
            buffer(chips, part_r), buffer(chips, own_b), buffer(chips, part_k),
            buffer(chips, part_r), buffer(chips, own_b), buffer(chips, part_k),
            buffer(chips, part_r), buffer(chips, own_b), buffer(chips, part_k),
            buffer(n_col, own_a),
            buffer(n_col, part_r),
            buffer(n_col, part_k),
            buffer(n_row, part_r),
            buffer(rows_i),
            buffer(chips, 2, 2, part_r),
            buffer(chips, 2, part_k),
            pltpu.SemaphoreType.DMA((rows_i // GROUP,)),
            pltpu.SemaphoreType.DMA((6, chips)),
            pltpu.SemaphoreType.DMA((6, chips)),
            pltpu.SemaphoreType.DMA((6,)),
            pltpu.SemaphoreType.DMA((6,)),
            pltpu.SemaphoreType.DMA((4, n_col)),
            pltpu.SemaphoreType.DMA((4, n_col)),
        ],
        compiler_params=pltpu.CompilerParams(
            collective_id=0, has_side_effects=True, vmem_limit_bytes=52 * 1024 * 1024
        ),
        cost_estimate=pl.CostEstimate(
            flops=4 * rows_i * rows_j * depth * rank,
            bytes_accessed=2 * rows_i * rows_j * depth,
            transcendentals=0,
        ),
    )(tensor, factor_a, factor_b, factor_c)
    return grad_a, grad_b, grad_c.reshape(depth, rank)


def solution(mesh):
    in_specs = (P("row", "col", None), P(("row", "col"), None), P(("col", "row"), None), P())
    out_specs = (P(("row", "col"), None), P(("col", "row"), None), P())
    body = functools.partial(shards, mesh.shape["row"], mesh.shape["col"])
    return jax.shard_map(body, mesh=mesh, in_specs=in_specs, out_specs=out_specs, check_vma=False)
```

```python
import functools

import jax
import jax.numpy as jnp
from jax import lax
from jax.experimental import pallas as pl
from jax.experimental.pallas import tpu as pltpu
from jax.sharding import PartitionSpec as P

MESH = pl.DeviceIdType.MESH
HIGHEST = lax.Precision.HIGHEST
GROUP = 8
WIDE = 32
BLOCKS = 5


def dot(left, right):
    return jnp.dot(left, right, precision=HIGHEST, preferred_element_type=jnp.float32)


def kernel(
    n_row, n_col, parts,
    t_hbm, fa_hbm, fb_hbm, fc_hbm,
    out_a, out_b, out_c,
    t_ref, x_ref, a_gather, b_gather, a_ref, fc_ref, c_low, gram_c,
    part_ga, part_mb, part_mc, mate_ga, mate_mb, mate_mc, half_ga, half_mb, half_mc,
    peer_ga, peer_mb, peer_mc, col_ma, col_gb, part_gb, part_ma, sums_ma,
    grams, final_c,
    load_sem, in_sem, row_send, row_recv, c_send, c_recv, mate_send, mate_recv, col_send, col_recv,
):
    row, col = lax.axis_index("row"), lax.axis_index("col")
    chips = n_row // 2
    chip, core = row // 2, lax.rem(row, 2)
    mate = {"row": row + 1 - 2 * core}
    rows_i, rows_j, depth = t_ref.shape
    rank = a_ref.shape[1]
    own_a, own_b = fa_hbm.shape[0], fb_hbm.shape[0]
    steps = rows_i // GROUP
    sends = []

    def chip_at(flip):
        other, bit = chip, 1
        while bit < chips:
            if flip & bit:
                other += bit * (1 - 2 * lax.rem(chip // bit, 2))
            bit *= 2
        return other

    def place(flip, shift):
        return chip_at(flip), lax.rem(col + shift, n_col)

    everyone = [(f, s) for f in range(chips) for s in range(n_col) if f or s]

    def send(source, target, send_sem, recv_sem, device):
        copy = pltpu.make_async_remote_copy(
            src_ref=source, dst_ref=target, send_sem=send_sem, recv_sem=recv_sem,
            device_id=device, device_id_type=MESH,
        )
        copy.start()
        sends.append(copy)
        return copy

    def across_row(phase, source, target):
        return [
            send(
                source(chip_at(flip)), target, row_send.at[phase, flip], row_recv.at[phase, flip],
                {"row": 2 * chip_at(flip) + core},
            )
            for flip in range(1, chips)
        ]

    def across_mate(phase, source, target):
        return send(source, target, mate_send.at[phase], mate_recv.at[phase], mate)

    def across_col(phase, source, target):
        return [
            send(
                source(place(0, shift)[1]), target,
                col_send.at[phase, shift], col_recv.at[phase, shift],
                {"col": place(0, shift)[1]},
            )
            for shift in range(1, n_col)
        ]

    def across_all(phase, reach, source, target):
        made = []
        for flip, shift in reach:
            other, other_col = place(flip, shift)
            made.append(send(
                source(other, other_col), target,
                c_send.at[phase, flip, shift], c_recv.at[phase, flip, shift],
                {"row": 2 * other + core, "col": other_col},
            ))
        return made

    def arrive(made):
        for copy in made:
            copy.wait_recv()

    def load(step):
        part = pl.ds(step * GROUP, GROUP)
        return pltpu.make_async_copy(t_hbm.at[part], t_ref.at[part], load_sem.at[step])

    barrier = pltpu.get_barrier_semaphore()
    pl.semaphore_signal(barrier, inc=1, device_id=mate, device_id_type=MESH)
    for flip, shift in everyone:
        other, other_col = place(flip, shift)
        pl.semaphore_signal(
            barrier, inc=1, device_id={"row": 2 * other + core, "col": other_col},
            device_id_type=MESH,
        )
    fc_load = pltpu.make_async_copy(fc_hbm, fc_ref, in_sem.at[0])
    fb_load = pltpu.make_async_copy(fb_hbm, b_gather.at[chip, core], in_sem.at[1])
    fa_load = pltpu.make_async_copy(fa_hbm, a_gather.at[col], in_sem.at[2])
    fc_load.start()
    fb_load.start()
    fa_load.start()
    for step in range(steps):
        load(step).start()

    def contract(begin, end):
        @pl.loop(begin, end)
        def _(step):
            load(step).wait()
            base = step * GROUP
            flat = t_ref[pl.ds(base, GROUP)].reshape(GROUP * rows_j, depth)
            product = jnp.dot(flat, c_low[...], preferred_element_type=jnp.float32)
            x_ref[pl.ds(base, GROUP)] = product.reshape(GROUP, rows_j, rank)

    def sum_over_i():
        @pl.loop(0, steps)
        def _(step):
            base = step * GROUP
            total = part_mb[...].reshape(rows_j, rank)
            for i in range(GROUP):
                total += x_ref[base + i] * a_ref[pl.ds(base + i, 1), :]
            part_mb[...] = total.reshape(part_mb.shape)

    width = 2 * own_b

    def use_block(other):
        begin = pl.multiple_of(other * width, width)
        b_part = b_gather[other].reshape(width, rank)

        @pl.loop(0, rows_i // WIDE)
        def _(step):
            base = step * WIDE
            panels = []
            for i in range(WIDE):
                a_row = a_ref[pl.ds(base + i, 1), :]
                panels.append((a_row * b_part).astype(jnp.bfloat16))
                terms = x_ref[base + i, pl.ds(begin, width), :] * b_part
                sums_ma[base + i] += jnp.sum(terms.reshape(width // 8, 8, rank), axis=0)
            panel = jnp.concatenate(panels, axis=0)
            flat = t_ref[pl.ds(base, WIDE), pl.ds(begin, width), :].reshape(WIDE * width, depth)
            product = lax.dot_general(
                flat, panel, (((0,), (0,)), ((), ())), preferred_element_type=jnp.float32
            )
            part_mc[...] += product.reshape(part_mc.shape)

    part_mb[...] = jnp.zeros_like(part_mb)
    part_mc[...] = jnp.zeros_like(part_mc)
    sums_ma[...] = jnp.zeros_like(sums_ma)
    fc_load.wait()
    factor_c = fc_ref[...]
    c_low[...] = factor_c.astype(jnp.bfloat16)
    gram_c[...] = dot(factor_c.T, factor_c)
    contract(0, steps // 2)
    fb_load.wait()
    fa_load.wait()
    pl.semaphore_wait(barrier, chips * n_col)

    b_moves = across_row(0, lambda other: b_gather.at[chip, core], b_gather.at[chip, core])
    b_mates = [across_mate(BLOCKS, b_gather.at[chip, core], b_gather.at[chip, core])]
    a_moves = across_col(0, lambda other: a_gather.at[col], a_gather.at[col])
    contract(steps // 2, steps)
    arrive(a_moves)
    a_block = a_gather[...].reshape(rows_i, rank)
    a_ref[...] = a_block
    part_ga[...] = dot(a_block.T, a_block).reshape(part_ga.shape)
    ga_mate = across_mate(0, part_ga.at[:, 1 - core], mate_ga)
    sum_over_i()
    mb_mate = across_mate(1, part_mb.at[:, 1 - core], mate_mb)
    arrive([ga_mate])
    half_ga[...] = part_ga[:, core] + mate_ga[...]
    ga_moves = across_row(1, lambda other: half_ga.at[other], peer_ga.at[chip])
    peer_ga[chip] = half_ga[chip]

    for flip in range(chips):
        if flip + 1 < chips:
            arrive([b_moves[flip]])
            view = b_gather.at[chip_at(flip + 1), core]
            b_mates.append(across_mate(BLOCKS + flip + 1, view, view))
        if flip == chips // 2:
            arrive([mb_mate])
            half_mb[...] = part_mb[:, core] + mate_mb[...]
            mb_moves = across_row(2, lambda other: half_mb.at[other], peer_mb.at[chip])
            peer_mb[chip] = half_mb[chip]
        arrive([b_mates[flip]])
        use_block(chip_at(flip))

    mc_mate = across_mate(2, part_mc.at[:, 1 - core], mate_mc)
    b_block = b_gather[...].reshape(rows_j, rank)
    part_gb[...] = dot(b_block.T, b_block).reshape(part_gb.shape)
    col_gb[col] = part_gb[row]
    gb_moves = across_col(1, lambda other: part_gb.at[row], col_gb.at[col])
    arrive([mc_mate])
    half_mc[...] = part_mc[:, core] + mate_mc[...]
    split = parts == n_col
    mc_moves = across_all(
        0, everyone,
        lambda other, other_col: half_mc.at[other, other_col if split else 0],
        peer_mc.at[chip, col],
    )
    mine = col if split else 0
    peer_mc[chip, col] = half_mc[chip, mine]
    part_ma[...] = jnp.sum(sums_ma[...], axis=1)
    ma_moves = across_col(
        2,
        lambda other: part_ma.at[pl.ds(pl.multiple_of(other * own_a, 8), own_a)],
        col_ma.at[col],
    )
    col_ma[col] = part_ma[pl.ds(pl.multiple_of(col * own_a, 8), own_a), :]
    arrive(ga_moves)
    arrive(gb_moves)
    gram_rows = [jnp.sum(peer_ga[...], axis=0), jnp.sum(col_gb[...], axis=0)]
    grams[chip, core] = jnp.stack(gram_rows)
    gram_moves = across_row(3, lambda other: grams.at[chip, core], grams.at[chip, core])
    arrive(mc_moves)
    pieces = peer_mc[...].reshape((chips * n_col,) + peer_mc.shape[2:])
    final_c[chip, core, mine] = jnp.sum(pieces, axis=0)
    reach = [(f, s) for f, s in everyone if split or s == 0]
    view = final_c.at[chip, core, mine]
    final_moves = across_all(1, reach, lambda other, other_col: view, view)
    arrive(mb_moves)
    arrive(ma_moves)
    arrive(gram_moves)
    gram_mate = across_mate(3, grams.at[:, core], grams.at[:, core])
    arrive([gram_mate])
    gram_a = grams[:, :, 0].reshape(rank, rank)
    gram_b = grams[:, :, 1].reshape(rank, rank)
    own_rows_a = a_gather[col]
    own_rows_b = b_gather[chip, core]
    out_a[...] = dot(own_rows_a, gram_b * gram_c[...]) - jnp.sum(col_ma[...], axis=0)
    out_b[...] = dot(own_rows_b, gram_a * gram_c[...]) - jnp.sum(peer_mb[...], axis=0)
    out_c[...] = dot(fc_ref[...], gram_a * gram_b).reshape(out_c.shape)
    arrive(final_moves)
    final_mate = across_mate(4, final_c.at[:, core], final_c.at[:, core])
    out_c[:, core] -= final_c[:, core]
    arrive([final_mate])
    out_c[:, 1 - core] -= final_c[:, 1 - core]
    for copy in sends:
        copy.wait_send()


def shards(n_row, n_col, tensor, factor_a, factor_b, factor_c):
    rows_i, rows_j, depth = tensor.shape
    own_a, rank = factor_a.shape
    own_b = factor_b.shape[0]
    chips = n_row // 2
    parts = n_col if depth % (8 * n_row * n_col) == 0 else 1
    part_r, part_k = rank // n_row, depth // (n_row * parts)
    f32 = jnp.float32

    def buffer(*shape):
        return pltpu.VMEM(shape + (rank,), f32)

    anywhere = pl.BlockSpec(memory_space=pl.ANY)
    vmem = pl.BlockSpec(memory_space=pltpu.VMEM)
    grad_a, grad_b, grad_c = pl.pallas_call(
        functools.partial(kernel, n_row, n_col, parts),
        out_shape=(
            jax.ShapeDtypeStruct((own_a, rank), f32),
            jax.ShapeDtypeStruct((own_b, rank), f32),
            jax.ShapeDtypeStruct((chips, 2, parts, part_k, rank), f32),
        ),
        in_specs=[anywhere] * 4,
        out_specs=(vmem, vmem, vmem),
        scratch_shapes=[
            pltpu.VMEM(tensor.shape, tensor.dtype),
            buffer(rows_i, rows_j),
            buffer(n_col, own_a),
            buffer(chips, 2, own_b),
            buffer(rows_i),
            buffer(depth),
            pltpu.VMEM((depth, rank), jnp.bfloat16),
            buffer(rank),
            buffer(chips, 2, part_r), buffer(chips, 2, own_b), buffer(chips, 2, parts, part_k),
            buffer(chips, part_r), buffer(chips, own_b), buffer(chips, parts, part_k),
            buffer(chips, part_r), buffer(chips, own_b), buffer(chips, parts, part_k),
            buffer(chips, part_r), buffer(chips, own_b), buffer(chips, n_col, part_k),
            buffer(n_col, own_a),
            buffer(n_col, part_r),
            buffer(n_row, part_r),
            buffer(rows_i),
            buffer(rows_i, 8),
            buffer(chips, 2, 2, part_r),
            buffer(chips, 2, parts, part_k),
            pltpu.SemaphoreType.DMA((rows_i // GROUP,)),
            pltpu.SemaphoreType.DMA((3,)),
            pltpu.SemaphoreType.DMA((4, chips)),
            pltpu.SemaphoreType.DMA((4, chips)),
            pltpu.SemaphoreType.DMA((2, chips, n_col)),
            pltpu.SemaphoreType.DMA((2, chips, n_col)),
            pltpu.SemaphoreType.DMA((BLOCKS + chips,)),
            pltpu.SemaphoreType.DMA((BLOCKS + chips,)),
            pltpu.SemaphoreType.DMA((3, n_col)),
            pltpu.SemaphoreType.DMA((3, n_col)),
        ],
        compiler_params=pltpu.CompilerParams(
            collective_id=0, has_side_effects=True, vmem_limit_bytes=52 * 1024 * 1024
        ),
        cost_estimate=pl.CostEstimate(
            flops=4 * rows_i * rows_j * depth * rank,
            bytes_accessed=2 * rows_i * rows_j * depth,
            transcendentals=0,
        ),
    )(tensor, factor_a, factor_b, factor_c)
    return grad_a, grad_b, grad_c.reshape(depth, rank)


def solution(mesh):
    in_specs = (P("row", "col", None), P(("row", "col"), None), P(("col", "row"), None), P())
    out_specs = (P(("row", "col"), None), P(("col", "row"), None), P())
    body = functools.partial(shards, mesh.shape["row"], mesh.shape["col"])
    return jax.shard_map(body, mesh=mesh, in_specs=in_specs, out_specs=out_specs, check_vma=False)
```
